32 devices in a mesh: dp: 4 (over y, core), tensor: 8 (over z, x).
Axes of the slice: x: 2, y: 2, z: 4, core: 2. Of those that a mesh axis runs over, the one named last changes fastest.
Arguments:
- thinker_rows: bfloat16 [8192, 8192], P('dp', 'tensor'), may hold values from -6 to 6
- proj_weight: bfloat16 [8192, 3584], P('tensor'), may hold values from -0.0625 to 0.0625
- proj_bias: float32 [3584], replicated, may hold values from -3 to 3
- cotangent: bfloat16 [8192, 3584], P('dp'), may hold values from -6 to 6
- block_owner: int32 [64], P('dp'), may hold values from 0 to 3, as said below
- block_offset: int32 [64], P('dp'), may hold values from 0 to 31, as said below
Outputs:
- grad_thinker: bfloat16 [16384, 8192], P('dp', 'tensor')
- proj_grad: float32 [8192, 3584], P(('tensor', 'dp'))
The draws below stay inside these ranges and needn't reach their ends.
Inputs may be any that keep to these rules, and one draw needn't show every extreme that they name: `block_owner`: the 16 blocks of one index of dp name at most 8 blocks for any one owner, and the blocks for one owner stand next to each other; one owner receives exactly 8 blocks from every index of dp. `block_offset`: no two talker blocks share both owner and offset.
All inputs are finite; a program needn't handle non-finite values.
Results may differ from the reference program's by a relative error of at most 0.015.
Values may be sent and summed in bfloat16 or wider, within the bound.
No kernel may reach another device: no remote copies, remote signals or barrier semaphores. Data moves between devices by JAX's collectives and lax.ppermute only.
A program may use at most 128 MiB of HBM per device.

```python
import jax
import jax.numpy as jnp
from jax import lax

D = 8192
E = 3584
BLOCK = 128
BLK_DEV = 16
OWN_BLK = 32
BLOCKS = 64
TOKENS = 8192
N_DP = 4
N_TENSOR = 8


def routing_tables(key):
    slot_cap = 2 * BLK_DEV // N_DP
    heavy_owner = jax.random.randint(jax.random.fold_in(key, 11), (), 0, N_DP)
    tickets = jnp.repeat(jnp.arange(N_DP, dtype=jnp.int32), slot_cap)

    def one_source(source):
        source_key = jax.random.fold_in(key, 100 + source)
        ticket_noise = jax.random.permutation(jax.random.fold_in(source_key, 1), tickets.shape[0]).astype(jnp.int32)
        ticket_score = jnp.where(tickets == heavy_owner, 0, 1 + ticket_noise)
        chosen = tickets[jnp.argsort(ticket_score)[:BLK_DEV]]
        owner_rank = jax.random.permutation(jax.random.fold_in(source_key, 2), N_DP).astype(jnp.int32)
        grouping = owner_rank[chosen] * BLK_DEV + jnp.arange(BLK_DEV, dtype=jnp.int32)
        return chosen[jnp.argsort(grouping)]
    owners = jax.vmap(one_source)(jnp.arange(N_DP, dtype=jnp.int32))
    owner_hot = (owners[:, :, None] == jnp.arange(N_DP, dtype=jnp.int32)[None, None, :]).astype(jnp.int32)
    within = jnp.sum((jnp.cumsum(owner_hot, axis=1) - owner_hot) * owner_hot, axis=2)
    linear = jnp.arange(N_DP, dtype=jnp.int32)[:, None] * slot_cap + within

    def one_shuffle(owner):
        return jax.random.permutation(jax.random.fold_in(key, 500 + owner), 2 * BLK_DEV).astype(jnp.int32)
    shuffles = jax.vmap(one_shuffle)(jnp.arange(N_DP, dtype=jnp.int32))
    offsets = shuffles[owners, linear]
    return (owners.reshape(-1).astype(jnp.int32), offsets.reshape(-1).astype(jnp.int32))


def draw_block_owner(key, part):
    return routing_tables(key)[0]


def draw_block_offset(key, part):
    return routing_tables(key)[1]


def spiked(drawn, rng, source, target, parts, factor):
    owner, partner = [(jnp.arange(drawn.shape[position]) // (drawn.shape[position] // parts)).reshape([-1 if axis == position else 1 for axis in range(drawn.ndim)]) for position in (source, target)]
    chosen = jax.random.permutation(rng, parts)[partner]
    strong = (owner == chosen) | (owner == (partner + parts // 2) % parts)
    return jnp.where(strong, factor * drawn, drawn)


def steps_of(stream_key, dims, shards, smallest, top_value):
    def one(dim, parts):
        draws = jax.random.uniform(jax.random.fold_in(jax.random.fold_in(stream_key, 6), dim), (parts,), jnp.float32, smallest / len(shards), top_value / len(shards))
        return jnp.repeat(jnp.exp(draws), dims[dim] // parts).reshape((-1,) + (1,) * (len(dims) - dim - 1))

    loudness = one(*shards[0])
    for cut in shards[1:]:
        loudness = loudness * one(*cut)
    return loudness


def centred(stream_key, dims, width, bound, pieces=(), held_as=jnp.bfloat16):
    array = jax.random.normal(stream_key, dims, jnp.float32) * width
    if len(pieces) > 0:
        array = steps_of(stream_key, dims, pieces, -0.22, 0.18) * array
    return jnp.clip(array, min=-bound, max=bound).astype(held_as)


def bell_draw_with(own_key, shape, spread, limit, cuts, heavy, held_as=jnp.bfloat16):
    drawn = spread * jax.random.normal(own_key, shape, jnp.float32)
    if cuts:
        drawn = drawn * steps_of(own_key, shape, cuts, -0.22, 0.18)
    return jnp.clip(spiked(drawn, jax.random.fold_in(own_key, 3), *heavy), -limit, limit).astype(held_as)


def setup_inputs(seed: int = 0) -> dict:
    key_list = jax.random.split(jax.random.key(seed), 7)
    return {
        "thinker_rows": bell_draw_with(key_list[0], (TOKENS, D), 1.0, 6.0, ((0, 4), (1, 8)), (0, 1, 8, 2.0)),
        "proj_weight": centred(key_list[1], (D, E), D ** -0.5, 0.0625, ((0, 8),)),
        "proj_bias": centred(key_list[2], (E,), 1.0, 3.0, (), jnp.float32),
        "cotangent": centred(key_list[3], (TOKENS, E), 1.0, 6.0, ((0, 4),)),
        "block_owner": draw_block_owner(jax.random.fold_in(key_list[6], 71), 0),
        "block_offset": draw_block_offset(jax.random.fold_in(key_list[6], 71), 0),
    }


def reference(thinker_rows, proj_weight, proj_bias, cotangent, block_owner, block_offset):
    local_width = D // N_TENSOR
    stacked_rows = thinker_rows.reshape(TOKENS, N_TENSOR, local_width).transpose(1, 0, 2)
    stacked_weight = proj_weight.reshape(N_TENSOR, local_width, E)

    def add_part(total, pair):
        partial_value = jnp.dot(pair[0], pair[1], preferred_element_type=jnp.float32)
        rounded = lax.optimization_barrier(partial_value.astype(jnp.bfloat16))
        return total + rounded.astype(jnp.float32), None

    summed, _ = lax.scan(add_part, jnp.zeros((TOKENS, E), jnp.float32), (stacked_rows, stacked_weight))
    pre_act = summed + proj_bias
    gate_value = jax.nn.sigmoid(pre_act)
    slope_rows = (cotangent.astype(jnp.float32) * gate_value * (1.0 + pre_act * (1.0 - gate_value))).astype(jnp.bfloat16)
    input_grad = jnp.dot(slope_rows, proj_weight.T, preferred_element_type=jnp.float32).astype(jnp.bfloat16)
    proj_grad = jnp.dot(thinker_rows.T, slope_rows, preferred_element_type=jnp.float32) * (TOKENS ** -0.5)
    target = (block_owner.astype(jnp.int32) * OWN_BLK + block_offset.astype(jnp.int32)).astype(jnp.int32)
    owner_grad = jnp.zeros((N_DP * OWN_BLK, BLOCK, D), jnp.bfloat16)
    owner_grad = owner_grad.at[target].set(input_grad.reshape(BLOCKS, BLOCK, D))
    return owner_grad.reshape(N_DP * OWN_BLK * BLOCK, D), proj_grad
```

```python
import jax
import jax.numpy as jnp
from jax import lax
from jax.experimental import pallas as pl
from jax.experimental.pallas import tpu as pltpu
from jax.sharding import PartitionSpec as P

BLOCK = 128
LANES = 256
F32 = jnp.float32
BF16 = jnp.bfloat16


def split_units(total, unit, parts):
    units = total // unit
    parts = min(parts, units)
    sizes = [units // parts] * parts
    middle = sorted(range(parts), key=lambda i: abs(2 * i - parts + 1))
    for i in middle[: units % parts]:
        sizes[i] += 1
    spans, start = [], 0
    for size in sizes:
        spans.append((start * unit, size * unit))
        start += size
    return spans


class Grid:
    def __init__(self, tensor_count, dp_count):
        self.nx = 1 << ((tensor_count.bit_length() - 1) // 2)
        self.nz = tensor_count // self.nx
        self.nc = 2
        self.ny = dp_count // self.nc
        t, d = lax.axis_index("tensor"), lax.axis_index("dp")
        self.z, self.x = t // self.nx, t % self.nx
        self.y, self.c = d // self.nc, d % self.nc
        self.d = d

    def swap_x(self, value, k):
        pairs = [(z * self.nx + x, z * self.nx + (x ^ k)) for z in range(self.nz) for x in range(self.nx)]
        return lax.ppermute(value, "tensor", pairs)

    def hop_z(self, value, h):
        moves = [(h, h + 1), (self.nz - 1 - h, self.nz - 2 - h)]
        pairs = [(a * self.nx + x, b * self.nx + x) for a, b in moves for x in range(self.nx)]
        return lax.ppermute(value, "tensor", pairs)

    def swap_y(self, value, k):
        pairs = [(y * self.nc + c, (y ^ k) * self.nc + c) for y in range(self.ny) for c in range(self.nc)]
        return lax.ppermute(value, "dp", pairs)

    def swap_core(self, value):
        return lax.ppermute(value, "dp", [(d, d ^ 1) for d in range(self.ny * self.nc)])


def rows_at(value, start, count):
    return lax.dynamic_slice_in_dim(value, start, count, 0)


def product(a, b, dims):
    return lax.dot_general(a, b, (dims, ((), ())), preferred_element_type=F32)


def place_blocks(pieces, piece_owner, piece_offset, taken, me, out_blocks, width):
    per = pieces[0].shape[0]
    count = len(pieces)

    def kernel(owner_ref, offset_ref, taken_ref, me_ref, *refs):
        sources, out_ref, zero_ref, sems, zero_sems = refs[:count], *refs[count:]
        zero_ref[...] = jnp.zeros_like(zero_ref)
        mine = me_ref[0]

        def copy(i, j):
            n = i * per + j
            return pltpu.make_async_copy(sources[i].at[j], out_ref.at[offset_ref[n]], sems.at[n])

        def clear(n):
            return pltpu.make_async_copy(zero_ref, out_ref.at[n], zero_sems.at[n])

        for i in range(count):
            for j in range(per):
                pl.when(owner_ref[i * per + j] == mine)(lambda: copy(i, j).start())
        for n in range(out_blocks):
            pl.when(taken_ref[n] == 0)(lambda: clear(n).start())
        for i in range(count):
            for j in range(per):
                pl.when(owner_ref[i * per + j] == mine)(lambda: copy(i, j).wait())
        for n in range(out_blocks):
            pl.when(taken_ref[n] == 0)(lambda: clear(n).wait())

    smem = pl.BlockSpec(memory_space=pltpu.SMEM)
    hbm = pl.BlockSpec(memory_space=pl.ANY)
    return pl.pallas_call(
        kernel,
        out_shape=jax.ShapeDtypeStruct((out_blocks, BLOCK, width), BF16),
        in_specs=[smem] * 4 + [hbm] * count,
        out_specs=hbm,
        scratch_shapes=[
            pltpu.VMEM((BLOCK, width), BF16),
            pltpu.SemaphoreType.DMA((count * per,)),
            pltpu.SemaphoreType.DMA((out_blocks,)),
        ],
        name="place_blocks",
    )(piece_owner, piece_offset, taken, me, *pieces)


def shards(thinker_rows, proj_weight, proj_bias, cotangent, block_owner, block_offset):
    g = Grid(lax.axis_size("tensor"), lax.axis_size("dp"))
    row_count, width = thinker_rows.shape
    dp_count = g.ny * g.nc
    out_width = proj_weight.shape[1]
    x_rows = row_count // g.nx
    x_blocks = x_rows // BLOCK
    nr = min(4, x_blocks)
    r_rows = x_rows // nr
    r_blocks = r_rows // BLOCK
    spans = split_units(out_width, LANES, 4)
    ne = len(spans)
    share = width // dp_count
    xs = range(1, g.nx)

    tables = lax.all_gather(jnp.stack([block_owner, block_offset]), "dp", axis=0)

    def weight_from_x(e):
        start, size = spans[e]
        mine = lax.dynamic_slice(proj_weight, (g.d * share, start), (share, size))
        whole = {}
        for k in xs:
            got = g.swap_x(mine, k)
            parts = {0: got}
            for ky in range(1, g.ny):
                parts[ky * g.nc] = g.swap_y(got, ky)
            for key in list(parts):
                parts[key ^ 1] = g.swap_core(parts[key])
            full = jnp.zeros((width, size), BF16)
            for key, part in parts.items():
                full = lax.dynamic_update_slice(full, part, ((g.d ^ key) * share, 0))
            whole[k] = full
        return whole

    def rows_from_x(r):
        return {k: g.swap_x(rows_at(thinker_rows, (g.x ^ k) * x_rows + r * r_rows, r_rows), k) for k in xs}

    own_rows = [rows_at(thinker_rows, g.x * x_rows + r * r_rows, r_rows) for r in range(nr)]
    own_weight = [proj_weight[:, start : start + size] for start, size in spans]
    x_weight = [None] * ne
    x_rows_got = [None] * nr
    x_weight[0] = weight_from_x(0)
    for r in range(nr):
        x_rows_got[r] = rows_from_x(r)
    for e in range(1, ne):
        x_weight[e] = weight_from_x(e)

    def slope_piece(r, e):
        start, size = spans[e]
        part = product(own_rows[r], own_weight[e], ((1,), (0,)))
        for k in xs:
            part = part + product(x_rows_got[r][k], x_weight[e][k], ((1,), (0,)))
        part = part.astype(BF16)
        total = part.astype(F32)
        send = part
        for h in range(g.nz - 1):
            got = g.hop_z(send, h).astype(F32)
            total = total + got
            send = (part.astype(F32) + got).astype(BF16)
        pre_act = total + proj_bias[start : start + size]
        gate = jax.nn.sigmoid(pre_act)
        cot = lax.dynamic_slice(cotangent, (g.x * x_rows + r * r_rows, start), (r_rows, size))
        return (cot.astype(F32) * gate * (1.0 + pre_act * (1.0 - gate))).astype(BF16)

    def weight_grad(e, pieces):
        slope = jnp.concatenate(pieces, axis=0)
        size = slope.shape[1]
        terms = {}
        for k in range(g.nx):
            left = jnp.concatenate([own_rows[r] if k == 0 else x_rows_got[r][k] for r in range(nr)], axis=0)
            term = product(left, slope, ((0,), (0,))).astype(BF16)
            term = term.reshape(g.ny, g.nc, share, size)
            keep = lax.dynamic_index_in_dim(term, g.c, 1, keepdims=False)
            give = lax.dynamic_index_in_dim(term, 1 - g.c, 1, keepdims=False)
            terms[k] = keep.astype(F32) + g.swap_core(give).astype(F32)
        total = terms[0]
        for k in xs:
            total = total + g.swap_x(terms[k].astype(BF16), k).astype(F32)
        mine = lax.dynamic_index_in_dim(total, g.y, 0, keepdims=False)
        for ky in range(1, g.ny):
            give = lax.dynamic_index_in_dim(total, g.y ^ ky, 0, keepdims=False).astype(BF16)
            mine = mine + g.swap_y(give, ky).astype(F32)
        return mine * float(row_count * dp_count) ** (-0.5)

    placed, placed_at = [], []

    def return_rows(r, pieces):
        slope = jnp.concatenate(pieces, axis=1)
        found = {}
        for k in range(g.nx):
            weight = proj_weight if k == 0 else jnp.concatenate([x_weight[e][k] for e in range(ne)], axis=1)
            grad = product(slope, weight, ((1,), (1,))).astype(BF16)
            found[(k, 0, 0)] = grad if k == 0 else g.swap_x(grad, k)
        for k in range(g.nx):
            for ky in range(1, g.ny):
                found[(k, ky, 0)] = g.swap_y(found[(k, 0, 0)], ky)
            for ky in range(g.ny):
                found[(k, ky, 1)] = g.swap_core(found[(k, ky, 0)])
        for (k, ky, kc), piece in found.items():
            placed.append(piece.reshape(r_blocks, BLOCK, width))
            placed_at.append((g.d ^ (ky * g.nc + kc), (g.x ^ k) * x_blocks + r * r_blocks))

    slopes = {}
    early = ne // 2
    order = [(r, e) for e in range(early) for r in range(nr)]
    order += [(r, e) for r in range(nr) for e in range(early, ne)]
    grads = [None] * ne
    for r, e in order:
        slopes[r, e] = slope_piece(r, e)
        if r == nr - 1:
            grads[e] = weight_grad(e, [slopes[i, e] for i in range(nr)])
        if e == ne - 1:
            return_rows(r, [slopes[r, i] for i in range(ne)])

    sources = jnp.stack([lax.dynamic_slice(tables, (d, 0, at), (1, 2, r_blocks))[0] for d, at in placed_at])
    piece_owner = sources[:, 0].reshape(-1)
    piece_offset = sources[:, 1].reshape(-1)
    out_blocks = 2 * row_count // BLOCK
    taken = jnp.any(
        (piece_owner == g.d)[None, :] & (piece_offset[None, :] == jnp.arange(out_blocks)[:, None]), axis=1
    ).astype(jnp.int32)
    grad_thinker = place_blocks(placed, piece_owner, piece_offset, taken, g.d[None], out_blocks, width)
    return grad_thinker.reshape(out_blocks * BLOCK, width), jnp.concatenate(grads, axis=1)


def solution(mesh):
    return jax.shard_map(
        shards,
        mesh=mesh,
        in_specs=(P("dp", "tensor"), P("tensor", None), P(), P("dp", None), P("dp"), P("dp")),
        out_specs=(P("dp", "tensor"), P(("tensor", "dp"), None)),
        check_vma=False,
    )
```

```python
import jax
import jax.numpy as jnp
from jax import lax
from jax.experimental import pallas as pl
from jax.experimental.pallas import tpu as pltpu
from jax.sharding import PartitionSpec as P

BLOCK = 128
LANES = 256
F32 = jnp.float32
BF16 = jnp.bfloat16
CUTS = (4 / 14, 8 / 14, 11 / 14)
GATHERED = 1
COST = 3.0


class Grid:
    def __init__(self, tensor_count, dp_count):
        self.nx = 1 << ((tensor_count.bit_length() - 1) // 2)
        self.nz = tensor_count // self.nx
        self.nc = 2
        self.ny = dp_count // self.nc
        t, d = lax.axis_index("tensor"), lax.axis_index("dp")
        self.z, self.x = t // self.nx, t % self.nx
        self.y, self.c = d // self.nc, d % self.nc
        self.d = d

    def swap_x(self, value, k):
        pairs = [(z * self.nx + x, z * self.nx + (x ^ k)) for z in range(self.nz) for x in range(self.nx)]
        return lax.ppermute(value, "tensor", pairs)

    def hop_z(self, value, h):
        moves = [(h, h + 1), (self.nz - 1 - h, self.nz - 2 - h)]
        pairs = [(a * self.nx + x, b * self.nx + x) for a, b in moves for x in range(self.nx)]
        return lax.ppermute(value, "tensor", pairs)

    def swap_y(self, value, k):
        pairs = [(y * self.nc + c, (y ^ k) * self.nc + c) for y in range(self.ny) for c in range(self.nc)]
        return lax.ppermute(value, "dp", pairs)

    def swap_core(self, value):
        return lax.ppermute(value, "dp", [(d, d ^ 1) for d in range(self.ny * self.nc)])


def rows_at(value, start, count):
    return lax.dynamic_slice_in_dim(value, start, count, 0)


SMALL = pl.CostEstimate(flops=1000, bytes_accessed=1000, transcendentals=0)


def work(flops):
    return pl.CostEstimate(flops=int(flops), bytes_accessed=1000, transcendentals=0)


PARAMS = pltpu.CompilerParams(vmem_limit_bytes=24 << 20)


def partial_product(rows, weights, starts, size):
    count, (height, width) = len(rows), rows[0].shape

    def kernel(*refs):
        total = jnp.dot(refs[0][...], refs[count][...], preferred_element_type=F32)
        for k in range(1, count):
            total += jnp.dot(refs[k][...], refs[count + k][...], preferred_element_type=F32)
        refs[-1][...] = total.astype(BF16)

    return pl.pallas_call(
        kernel,
        grid=(size // LANES,),
        out_shape=jax.ShapeDtypeStruct((height, size), BF16),
        in_specs=[pl.BlockSpec((height, width), lambda j: (0, 0))] * count
        + [pl.BlockSpec((width, LANES), lambda j, u=s // LANES: (0, u + j)) for s in starts],
        out_specs=pl.BlockSpec((height, LANES), lambda j: (0, j)),
        compiler_params=PARAMS,
        cost_estimate=work(COST * 2 * count * height * width * size),
        name="partial_product",
    )(*rows, *weights)


def return_product(slopes, weights):
    count, height = len(slopes), slopes[0].shape[0]
    sizes = [s.shape[1] for s in slopes]
    width = weights[0].shape[0]
    tile = min(LANES, width)
    places, at = [], 0
    for i, w in enumerate(weights):
        places += [(i, at, c) for c in (0,)]
        at += w.shape[1]

    def columns(refs, start, size):
        for i, first, _ in places:
            if first <= start < first + weights[i].shape[1]:
                return refs[count + i][:, start - first : start - first + size]

    def kernel(*refs):
        total, start = None, 0
        for i, size in enumerate(sizes):
            weight = columns(refs, start, size)
            term = lax.dot_general(refs[i][...], weight, (((1,), (1,)), ((), ())), preferred_element_type=F32)
            total = term if total is None else total + term
            start += size
        refs[-1][...] = total.astype(BF16)

    return pl.pallas_call(
        kernel,
        grid=(width // tile,),
        out_shape=jax.ShapeDtypeStruct((height, width), BF16),
        in_specs=[pl.BlockSpec((height, size), lambda j: (0, 0)) for size in sizes]
        + [pl.BlockSpec((tile, w.shape[1]), lambda j: (j, 0)) for w in weights],
        out_specs=pl.BlockSpec((height, tile), lambda j: (0, j)),
        compiler_params=PARAMS,
        cost_estimate=work(COST * 2 * height * width * sum(sizes)),
        name="return_product",
    )(*slopes, *weights)


def grad_product(half, turned, slopes, extra, kinds):
    groups, count = len(turned), len(slopes)
    height, size = slopes[0].shape
    ny, nc, share, rows = turned[0].shape
    more = 0 if extra is None else groups

    def kernel(half_ref, *refs):
        pieces = refs[groups : groups + count]
        for k in range(groups):
            left = refs[k][...].reshape(ny * share, rows)
            total = None
            for i in range(count):
                term = jnp.dot(left[:, i * height : (i + 1) * height], pieces[i][...], preferred_element_type=F32)
                total = term if total is None else total + term
            total = total.reshape(ny, share, LANES)
            if more:
                total = total + refs[groups + count + k][...].astype(F32)
            out = refs[groups + count + more + k]
            out[...] = total.astype(out.dtype)

    column = pl.BlockSpec((ny, share, LANES), lambda j, h: (0, 0, j))
    return pl.pallas_call(
        kernel,
        grid_spec=pltpu.PrefetchScalarGridSpec(
            num_scalar_prefetch=1,
            grid=(size // LANES,),
            in_specs=[pl.BlockSpec((ny, None, share, rows), lambda j, h: (0, h[0], 0, 0))] * groups
            + [pl.BlockSpec((height, LANES), lambda j, h: (0, j))] * count
            + [column] * more,
            out_specs=[column] * groups,
        ),
        out_shape=[jax.ShapeDtypeStruct((ny, share, size), kind) for kind in kinds],
        compiler_params=PARAMS,
        cost_estimate=work(COST * 2 * groups * ny * share * rows * size),
        name="grad_product",
    )(half, *turned, *slopes, *([] if extra is None else extra))


def place_blocks(out, pieces, owner, offset, taken, me, out_blocks, width):
    where = [(i, j) for i, piece in enumerate(pieces) for j in range(piece.shape[0])]
    count, total = len(pieces), len(where)
    first = out is None

    def kernel(owner_ref, offset_ref, taken_ref, me_ref, *refs):
        sources, (out_ref, stage, zero, in_sems, out_sems, zero_sems) = refs[:count], refs[-6:]
        mine = me_ref[0]

        def arrive(n):
            i, j = where[n]
            return pltpu.make_async_copy(sources[i].at[j], stage.at[n], in_sems.at[n])

        def leave(n):
            return pltpu.make_async_copy(stage.at[n], out_ref.at[offset_ref[n]], out_sems.at[n])

        def clear(n):
            return pltpu.make_async_copy(zero, out_ref.at[n], zero_sems.at[n])

        def each(work):
            for n in range(total):
                pl.when(owner_ref[n] == mine)(lambda: work(n))

        def forward(n):
            arrive(n).wait()
            leave(n).start()

        each(lambda n: arrive(n).start())
        if first:
            zero[...] = jnp.zeros_like(zero)
            for n in range(out_blocks):
                pl.when(taken_ref[n] == 0)(lambda: clear(n).start())
        each(forward)
        each(lambda n: leave(n).wait())
        if first:
            for n in range(out_blocks):
                pl.when(taken_ref[n] == 0)(lambda: clear(n).wait())

    smem = pl.BlockSpec(memory_space=pltpu.SMEM)
    hbm = pl.BlockSpec(memory_space=pl.ANY)
    before = [] if first else [out]
    return pl.pallas_call(
        kernel,
        out_shape=jax.ShapeDtypeStruct((out_blocks, BLOCK, width), BF16),
        in_specs=[smem] * 4 + [hbm] * (count + len(before)),
        out_specs=hbm,
        scratch_shapes=[
            pltpu.VMEM((total, BLOCK, width), BF16),
            pltpu.VMEM((BLOCK, width), BF16),
            pltpu.SemaphoreType.DMA((total,)),
            pltpu.SemaphoreType.DMA((total,)),
            pltpu.SemaphoreType.DMA((out_blocks,)),
        ],
        input_output_aliases={} if first else {4 + count: 0},
        compiler_params=PARAMS,
        cost_estimate=SMALL,
        name="place_blocks",
    )(owner, offset, taken, me, *pieces, *before)


class Order:
    def __init__(self):
        self.last = None

    def pin(self, value):
        if self.last is not None:
            value, _ = lax.optimization_barrier((value, self.last))
        return value

    def done(self, value):
        self.last = value
        return value


def shards(thinker_rows, proj_weight, proj_bias, cotangent, block_owner, block_offset):
    g = Grid(lax.axis_size("tensor"), lax.axis_size("dp"))
    row_count, width = thinker_rows.shape
    dp_count = g.ny * g.nc
    out_width = proj_weight.shape[1]
    x_rows = row_count // g.nx
    x_blocks = x_rows // BLOCK
    nr = min(2, x_blocks)
    r_rows = x_rows // nr
    r_blocks = r_rows // BLOCK
    units = out_width // LANES
    ends = [0] + [round(units * f) * LANES for f in CUTS] + [out_width]
    spans = list(zip(ends[:-1], ends[1:]))
    ne = len(spans)
    loads = [spans[0], spans[1], (spans[2][0], out_width)]
    share = width // dp_count
    xs = range(1, g.nx)
    out_blocks = 2 * row_count // BLOCK
    line = Order()
    later = {}

    def at(tick, work):
        later.setdefault(tick, []).append(work)

    x_weight, x_rows_got = {}, {}

    def load_of(e):
        return min(e, len(loads) - 1)

    def load_weight(i):
        start, end = loads[i]
        mine = lax.dynamic_slice(proj_weight, (line.pin(g.d * share), start), (share, end - start))
        for k in xs:
            x_weight[i, k] = g.swap_x(mine, k)

    def share_far(i):
        for k in xs:
            got = line.pin(x_weight[i, k])
            parts = {ky * g.nc: g.swap_y(got, ky) for ky in range(1, g.ny)}
            parts[0], parts[1] = got, g.swap_core(got)
            x_weight[i, k] = parts

    def share_near(i):
        for k in xs:
            parts = x_weight[i, k]
            for ky in range(1, g.ny):
                key = ky * g.nc
                parts[key] = line.pin(parts[key])
                parts[key + 1] = g.swap_core(parts[key])
            full = jnp.zeros((width, loads[i][1] - loads[i][0]), BF16)
            for key, part in sorted(parts.items()):
                full = lax.dynamic_update_slice(full, part, ((g.d ^ key) * share, 0))
            x_weight[i, k] = line.done(full)

    def share_all(i):
        for k in xs:
            x_weight[i, k] = lax.all_gather(line.pin(x_weight[i, k]), "dp", axis=0, tiled=True)

    def load_rows(r):
        for k in xs:
            mine = rows_at(thinker_rows, (line.pin(g.x) ^ k) * x_rows + r * r_rows, r_rows)
            x_rows_got[r, k] = g.swap_x(mine, k)

    own_rows = [None] * nr
    own_weight = [None] * ne
    turned = {}

    def turn(k, value):
        turned[k] = line.done(value.T.reshape(g.ny, g.nc, share, x_rows))

    def add_up(part, got):
        return line.done((line.pin(part).astype(F32) + got.astype(F32)).astype(BF16))

    partials, hops, slopes = {}, {}, {}

    def partial_of(r, e):
        start, end = spans[e]
        rows = [line.pin(own_rows[r])] + [x_rows_got[r, k] for k in xs]
        i = load_of(e)
        weights = [own_weight[e]] + [x_weight[i, k] for k in xs]
        part = line.done(partial_product(rows, weights, [0] + [start - loads[i][0]] * len(xs), end - start))
        partials[r, e] = part
        hops[r, e] = [g.hop_z(part, 0)]

    def hop(r, e, h):
        hops[r, e].append(g.hop_z(add_up(partials[r, e], hops[r, e][-1]), h))

    def slope_of(r, e):
        start, end = spans[e]
        total = line.pin(partials[r, e]).astype(F32)
        for got in hops[r, e]:
            total = total + got.astype(F32)
        pre_act = total + proj_bias[start:end]
        gate = jax.nn.sigmoid(pre_act)
        cot = lax.dynamic_slice(cotangent, (g.x * x_rows + r * r_rows, start), (r_rows, end - start))
        slopes[r, e] = line.done((cot.astype(F32) * gate * (1.0 + pre_act * (1.0 - gate))).astype(BF16))

    grads = [None] * ne
    half = g.c.astype(jnp.int32)[None]

    def weight_grad(e, tick):
        pieces = [line.pin(slopes[0, e])] + [slopes[r, e] for r in range(1, nr)]
        groups = list(xs) + [0]
        give = grad_product(1 - half, [turned[k] for k in groups], pieces, None, [BF16] * g.nx)
        line.done(give[0])
        got = {k: g.swap_core(v) for k, v in zip(groups, give)}

        def over_x():
            x_got = []
            for k in xs:
                value = grad_product(line.pin(half), [turned[k]], pieces, [got[k]], [BF16])[0]
                x_got.append(g.swap_x(line.done(value), k))
            mine = line.done(grad_product(line.pin(half), [turned[0]], pieces, [got[0]], [F32])[0])

            def over_y():
                total = line.pin(mine)
                for v in x_got:
                    total = total + v.astype(F32)
                total = line.done(total)
                own = lax.dynamic_index_in_dim(total, g.y, 0, keepdims=False)
                y_got = [
                    g.swap_y(lax.dynamic_index_in_dim(total, g.y ^ ky, 0, keepdims=False).astype(BF16), ky)
                    for ky in range(1, g.ny)
                ]

                def finish():
                    value = line.pin(own)
                    for v in y_got:
                        value = value + v.astype(F32)
                    grads[e] = line.done(value * float(row_count * dp_count) ** (-0.5))

                at(tick + 6, finish)

            at(tick + 4, over_y)

        at(tick + 1, over_x)

    state = {"out": None}

    def return_rows(r, tick, gathered):
        grad, placed, placed_at = {}, [], []
        pieces = [slopes[r, e] for e in range(ne)]

        def multiply(k):
            weights = [proj_weight] if k == 0 else [x_weight[i, k] for i in range(len(loads))]
            grad[k] = line.done(return_product([line.pin(pieces[0])] + pieces[1:], weights))

        for k in xs:
            multiply(k)
            grad[k] = g.swap_x(grad[k], k)
        multiply(0)

        def keep_piece(piece, k, ky, kc):
            placed.append(piece.reshape(r_blocks, BLOCK, width))
            placed_at.append((g.d ^ (ky * g.nc + kc), (g.x ^ k) * x_blocks + r * r_blocks))

        def everywhere(k):
            piece = lax.all_gather(line.pin(grad[k]), "dp", axis=0, tiled=True)
            placed.append(piece.reshape(dp_count * r_blocks, BLOCK, width))
            placed_at.extend((s, (g.x ^ k) * x_blocks + r * r_blocks) for s in range(dp_count))

        def spread(k):
            piece = line.pin(grad[k])
            across = [g.swap_y(piece, ky) for ky in range(1, g.ny)]
            keep_piece(piece, k, 0, 0)
            keep_piece(g.swap_core(piece), k, 0, 1)

            def other_core():
                for ky in range(1, g.ny):
                    piece = line.pin(across[ky - 1])
                    keep_piece(piece, k, ky, 0)
                    keep_piece(g.swap_core(piece), k, ky, 1)

            return other_core

        def place():
            sources = jnp.stack(
                [lax.dynamic_slice(tables, (s, 0, t), (1, 2, r_blocks))[0] for s, t in placed_at]
            )
            owner, offset = sources[:, 0].reshape(-1), sources[:, 1].reshape(-1)
            pieces = [line.pin(placed[0])] + placed[1:]
            state["out"] = line.done(
                place_blocks(state["out"], pieces, owner, offset, taken, g.d[None], out_blocks, width)
            )

        if gathered:
            everywhere(0)
            at(tick + 1, lambda: [everywhere(k) for k in xs])
            at(tick + 5, place)
        else:
            own_next = spread(0)

            def after_x():
                for k in xs:
                    at(tick + 3, spread(k))
                at(tick + 4, place)

            at(tick + 1, after_x)
            at(tick + 2, own_next)

    load_weight(0)
    tables = lax.all_gather(jnp.stack([block_owner, block_offset]), "dp", axis=0)
    own_rows[0] = line.done(rows_at(thinker_rows, g.x * x_rows, r_rows))
    load_rows(0)
    mine = line.pin(tables[:, 0]) == g.d
    reached = mine[:, :, None] & (tables[:, 1][:, :, None] == jnp.arange(out_blocks))
    taken = line.done(jnp.any(reached, axis=(0, 1)).astype(jnp.int32))
    share_far(0)
    line.done(x_weight[0, xs[0]][0] if xs else taken)
    for r in range(1, nr):
        load_rows(r)
    for r in range(1, nr):
        own_rows[r] = rows_at(thinker_rows, line.pin(g.x) * x_rows + r * r_rows, r_rows)
    line.done(own_rows[-1])
    turn(0, rows_at(thinker_rows, line.pin(g.x) * x_rows, x_rows))
    own_weight[0] = line.done(line.pin(proj_weight[:, spans[0][0] : spans[0][1]]))
    share_near(0)

    chunks = [(r, 0) for r in range(nr)] + [(0, e) for e in range(1, ne)]
    chunks += [(r, e) for r in range(1, nr) for e in range(1, ne)]
    before = {
        1: [lambda: share_near(1)],
        2: [lambda: share_near(2)],
        3: [
            lambda: [
                turn(k, jnp.concatenate([line.pin(x_rows_got[0, k])] + [x_rows_got[r, k] for r in range(1, nr)], axis=0))
                for k in xs
            ]
        ],
    }

    def own_columns(e):
        own_weight[e] = line.done(line.pin(proj_weight[:, spans[e][0] : spans[e][1]]))

    at(0, lambda: load_weight(2))
    at(0, lambda: own_columns(1))
    at(0, lambda: share_far(1))
    at(1, lambda: share_far(2))
    at(1, lambda: [own_columns(e) for e in range(2, ne)])
    partial_of(*chunks[0])
    load_weight(1)
    tick = 0
    hop_count = g.nz - 1

    def hop_all():
        for h in range(1, hop_count):
            if 0 <= tick - h + 1 < len(chunks):
                hop(*chunks[tick - h + 1], h)

    while tick < len(chunks) + hop_count or any(t >= tick for t in later):
        early = False
        if early:
            hop_all()
        for work in before.get(tick, []):
            work()
        if tick + 1 < len(chunks):
            partial_of(*chunks[tick + 1])
        if not early:
            hop_all()
        ready = tick - hop_count + 1
        if 0 <= ready < len(chunks):
            r, e = chunks[ready]
            slope_of(r, e)
            if all((r, j) in slopes for j in range(ne)):
                return_rows(r, tick, r < GATHERED)
            if all((j, e) in slopes for j in range(nr)):
                weight_grad(e, tick)
        for work in later.pop(tick, []):
            work()
        tick += 1

    return state["out"].reshape(out_blocks * BLOCK, width), jnp.concatenate(grads, axis=1)


def solution(mesh):
    return jax.shard_map(
        shards,
        mesh=mesh,
        in_specs=(P("dp", "tensor"), P("tensor", None), P(), P("dp", None), P("dp"), P("dp")),
        out_specs=(P("dp", "tensor"), P(("tensor", "dp"), None)),
        check_vma=False,
    )
```

```python
import jax
import jax.numpy as jnp
from jax import lax
from jax.experimental import pallas as pl
from jax.experimental.pallas import tpu as pltpu
from jax.sharding import PartitionSpec as P

BLOCK = 128
LANES = 256
F32 = jnp.float32
BF16 = jnp.bfloat16
CUTS = (4 / 14, 8 / 14, 11 / 14)
GATHERED = 1
COST = 8.0
TAIL = 8.0


class Grid:
    def __init__(self, tensor_count, dp_count):
        self.nx = 1 << ((tensor_count.bit_length() - 1) // 2)
        self.nz = tensor_count // self.nx
        self.nc = 2
        self.ny = dp_count // self.nc
        t, d = lax.axis_index("tensor"), lax.axis_index("dp")
        self.z, self.x = t // self.nx, t % self.nx
        self.y, self.c = d // self.nc, d % self.nc
        self.d = d

    def swap_x(self, value, k):
        pairs = [(z * self.nx + x, z * self.nx + (x ^ k)) for z in range(self.nz) for x in range(self.nx)]
        return lax.ppermute(value, "tensor", pairs)

    def hop_z(self, value, h):
        moves = [(h, h + 1), (self.nz - 1 - h, self.nz - 2 - h)]
        pairs = [(a * self.nx + x, b * self.nx + x) for a, b in moves for x in range(self.nx)]
        return lax.ppermute(value, "tensor", pairs)

    def swap_y(self, value, k):
        pairs = [(y * self.nc + c, (y ^ k) * self.nc + c) for y in range(self.ny) for c in range(self.nc)]
        return lax.ppermute(value, "dp", pairs)

    def swap_core(self, value):
        return lax.ppermute(value, "dp", [(d, d ^ 1) for d in range(self.ny * self.nc)])


def rows_at(value, start, count):
    return lax.dynamic_slice_in_dim(value, start, count, 0)


SMALL = pl.CostEstimate(flops=1000, bytes_accessed=1000, transcendentals=0)


PACE = [COST]


def work(flops):
    return pl.CostEstimate(flops=int(PACE[0] * flops), bytes_accessed=1000, transcendentals=0)


PARAMS = pltpu.CompilerParams(vmem_limit_bytes=24 << 20)


def partial_product(rows, weights, starts, size):
    count, (height, width) = len(rows), rows[0].shape

    def kernel(*refs):
        total = jnp.dot(refs[0][...], refs[count][...], preferred_element_type=F32)
        for k in range(1, count):
            total += jnp.dot(refs[k][...], refs[count + k][...], preferred_element_type=F32)
        refs[-1][...] = total.astype(BF16)

    return pl.pallas_call(
        kernel,
        grid=(size // LANES,),
        out_shape=jax.ShapeDtypeStruct((height, size), BF16),
        in_specs=[pl.BlockSpec((height, width), lambda j: (0, 0))] * count
        + [pl.BlockSpec((width, LANES), lambda j, u=s // LANES: (0, u + j)) for s in starts],
        out_specs=pl.BlockSpec((height, LANES), lambda j: (0, j)),
        compiler_params=PARAMS,
        cost_estimate=work(2 * count * height * width * size),
        name="partial_product",
    )(*rows, *weights)


def return_product(slopes, weights):
    count, height = len(slopes), slopes[0].shape[0]
    sizes = [s.shape[1] for s in slopes]
    width = weights[0].shape[0]
    tile = min(LANES, width)
    places, at = [], 0
    for i, w in enumerate(weights):
        places += [(i, at, c) for c in (0,)]
        at += w.shape[1]

    def columns(refs, start, size):
        for i, first, _ in places:
            if first <= start < first + weights[i].shape[1]:
                return refs[count + i][:, start - first : start - first + size]

    def kernel(*refs):
        total, start = None, 0
        for i, size in enumerate(sizes):
            weight = columns(refs, start, size)
            term = lax.dot_general(refs[i][...], weight, (((1,), (1,)), ((), ())), preferred_element_type=F32)
            total = term if total is None else total + term
            start += size
        refs[-1][...] = total.astype(BF16)

    return pl.pallas_call(
        kernel,
        grid=(width // tile,),
        out_shape=jax.ShapeDtypeStruct((height, width), BF16),
        in_specs=[pl.BlockSpec((height, size), lambda j: (0, 0)) for size in sizes]
        + [pl.BlockSpec((tile, w.shape[1]), lambda j: (j, 0)) for w in weights],
        out_specs=pl.BlockSpec((height, tile), lambda j: (0, j)),
        compiler_params=PARAMS,
        cost_estimate=work(2 * height * width * sum(sizes)),
        name="return_product",
    )(*slopes, *weights)


def grad_product(half, turned, slopes, extra, kinds):
    groups, count = len(turned), len(slopes)
    height, size = slopes[0].shape
    ny, nc, share, rows = turned[0].shape
    more = 0 if extra is None else groups

    def kernel(half_ref, *refs):
        pieces = refs[groups : groups + count]
        for k in range(groups):
            left = refs[k][...].reshape(ny * share, rows)
            total = None
            for i in range(count):
                term = jnp.dot(left[:, i * height : (i + 1) * height], pieces[i][...], preferred_element_type=F32)
                total = term if total is None else total + term
            total = total.reshape(ny, share, LANES)
            if more:
                total = total + refs[groups + count + k][...].astype(F32)
            out = refs[groups + count + more + k]
            out[...] = total.astype(out.dtype)

    column = pl.BlockSpec((ny, share, LANES), lambda j, h: (0, 0, j))
    return pl.pallas_call(
        kernel,
        grid_spec=pltpu.PrefetchScalarGridSpec(
            num_scalar_prefetch=1,
            grid=(size // LANES,),
            in_specs=[pl.BlockSpec((ny, None, share, rows), lambda j, h: (0, h[0], 0, 0))] * groups
            + [pl.BlockSpec((height, LANES), lambda j, h: (0, j))] * count
            + [column] * more,
            out_specs=[column] * groups,
        ),
        out_shape=[jax.ShapeDtypeStruct((ny, share, size), kind) for kind in kinds],
        compiler_params=PARAMS,
        cost_estimate=work(2 * groups * ny * share * rows * size),
        name="grad_product",
    )(half, *turned, *slopes, *([] if extra is None else extra))


def place_blocks(out, pieces, owner, offset, taken, me, out_blocks, width):
    where = [(i, j) for i, piece in enumerate(pieces) for j in range(piece.shape[0])]
    count, total = len(pieces), len(where)
    first = out is None

    def kernel(owner_ref, offset_ref, taken_ref, me_ref, *refs):
        sources, (out_ref, stage, zero, in_sems, out_sems, zero_sems) = refs[:count], refs[-6:]
        mine = me_ref[0]

        def arrive(n):
            i, j = where[n]
            return pltpu.make_async_copy(sources[i].at[j], stage.at[n], in_sems.at[n])

        def leave(n):
            return pltpu.make_async_copy(stage.at[n], out_ref.at[offset_ref[n]], out_sems.at[n])

        def clear(n):
            return pltpu.make_async_copy(zero, out_ref.at[n], zero_sems.at[n])

        def each(work):
            for n in range(total):
                pl.when(owner_ref[n] == mine)(lambda: work(n))

        def forward(n):
            arrive(n).wait()
            leave(n).start()

        each(lambda n: arrive(n).start())
        if first:
            zero[...] = jnp.zeros_like(zero)
            for n in range(out_blocks):
                pl.when(taken_ref[n] == 0)(lambda: clear(n).start())
        each(forward)
        each(lambda n: leave(n).wait())
        if first:
            for n in range(out_blocks):
                pl.when(taken_ref[n] == 0)(lambda: clear(n).wait())

    smem = pl.BlockSpec(memory_space=pltpu.SMEM)
    hbm = pl.BlockSpec(memory_space=pl.ANY)
    before = [] if first else [out]
    return pl.pallas_call(
        kernel,
        out_shape=jax.ShapeDtypeStruct((out_blocks, BLOCK, width), BF16),
        in_specs=[smem] * 4 + [hbm] * (count + len(before)),
        out_specs=hbm,
        scratch_shapes=[
            pltpu.VMEM((total, BLOCK, width), BF16),
            pltpu.VMEM((BLOCK, width), BF16),
            pltpu.SemaphoreType.DMA((total,)),
            pltpu.SemaphoreType.DMA((total,)),
            pltpu.SemaphoreType.DMA((out_blocks,)),
        ],
        input_output_aliases={} if first else {4 + count: 0},
        compiler_params=PARAMS,
        cost_estimate=SMALL,
        name="place_blocks",
    )(owner, offset, taken, me, *pieces, *before)


class Order:
    def __init__(self):
        self.last = None

    def pin(self, value):
        if self.last is not None:
            value, _ = lax.optimization_barrier((value, self.last))
        return value

    def done(self, value):
        self.last = value
        return value


def shards(thinker_rows, proj_weight, proj_bias, cotangent, block_owner, block_offset):
    g = Grid(lax.axis_size("tensor"), lax.axis_size("dp"))
    row_count, width = thinker_rows.shape
    dp_count = g.ny * g.nc
    out_width = proj_weight.shape[1]
    x_rows = row_count // g.nx
    x_blocks = x_rows // BLOCK
    nr = min(2, x_blocks)
    r_rows = x_rows // nr
    r_blocks = r_rows // BLOCK
    units = out_width // LANES
    ends = [0] + [round(units * f) * LANES for f in CUTS] + [out_width]
    spans = list(zip(ends[:-1], ends[1:]))
    ne = len(spans)
    loads = [spans[0], spans[1], (spans[2][0], out_width)]
    share = width // dp_count
    xs = range(1, g.nx)
    out_blocks = 2 * row_count // BLOCK
    line = Order()
    later = {}

    def at(tick, work):
        later.setdefault(tick, []).append(work)

    x_weight, x_rows_got = {}, {}

    def load_of(e):
        return min(e, len(loads) - 1)

    def load_weight(i):
        start, end = loads[i]
        mine = lax.dynamic_slice(proj_weight, (line.pin(g.d * share), start), (share, end - start))
        for k in xs:
            x_weight[i, k] = g.swap_x(mine, k)

    def share_far(i):
        for k in xs:
            got = line.pin(x_weight[i, k])
            parts = {ky * g.nc: g.swap_y(got, ky) for ky in range(1, g.ny)}
            parts[0], parts[1] = got, g.swap_core(got)
            x_weight[i, k] = parts

    def share_near(i):
        for k in xs:
            parts = x_weight[i, k]
            for ky in range(1, g.ny):
                key = ky * g.nc
                parts[key] = line.pin(parts[key])
                parts[key + 1] = g.swap_core(parts[key])
            full = jnp.zeros((width, loads[i][1] - loads[i][0]), BF16)
            for key, part in sorted(parts.items()):
                full = lax.dynamic_update_slice(full, part, ((g.d ^ key) * share, 0))
            x_weight[i, k] = line.done(full)

    def share_all(i):
        for k in xs:
            x_weight[i, k] = lax.all_gather(line.pin(x_weight[i, k]), "dp", axis=0, tiled=True)

    def load_rows(r):
        for k in xs:
            mine = rows_at(thinker_rows, (line.pin(g.x) ^ k) * x_rows + r * r_rows, r_rows)
            x_rows_got[r, k] = g.swap_x(mine, k)

    own_rows = [None] * nr
    own_weight = [None] * ne
    turned = {}

    def turn(k, value):
        turned[k] = line.done(value.T.reshape(g.ny, g.nc, share, x_rows))

    def add_up(part, got):
        return line.done((line.pin(part).astype(F32) + got.astype(F32)).astype(BF16))

    partials, hops, slopes = {}, {}, {}

    def partial_of(r, e):
        start, end = spans[e]
        rows = [line.pin(own_rows[r])] + [x_rows_got[r, k] for k in xs]
        i = load_of(e)
        weights = [own_weight[e]] + [x_weight[i, k] for k in xs]
        part = line.done(partial_product(rows, weights, [0] + [start - loads[i][0]] * len(xs), end - start))
        partials[r, e] = part
        hops[r, e] = [g.hop_z(part, 0)]

    def hop(r, e, h):
        hops[r, e].append(g.hop_z(add_up(partials[r, e], hops[r, e][-1]), h))

    def slope_of(r, e):
        start, end = spans[e]
        total = line.pin(partials[r, e]).astype(F32)
        for got in hops[r, e]:
            total = total + got.astype(F32)
        pre_act = total + proj_bias[start:end]
        gate = jax.nn.sigmoid(pre_act)
        cot = lax.dynamic_slice(cotangent, (g.x * x_rows + r * r_rows, start), (r_rows, end - start))
        slopes[r, e] = line.done((cot.astype(F32) * gate * (1.0 + pre_act * (1.0 - gate))).astype(BF16))

    grads = [None] * ne
    half = g.c.astype(jnp.int32)[None]

    def weight_grad(e):
        pieces = [slopes[r, e] for r in range(nr)]
        groups = list(xs) + [0]
        held = {}

        def over_core():
            give = grad_product(
                1 - half, [turned[k] for k in groups], [line.pin(pieces[0])] + pieces[1:], None, [BF16] * g.nx
            )
            line.done(give[0])
            held["core"] = {k: g.swap_core(v) for k, v in zip(groups, give)}

        def over_x():
            got = held["core"]
            held["x"] = []
            for k in xs:
                value = grad_product(line.pin(half), [turned[k]], pieces, [got[k]], [BF16])[0]
                held["x"].append(g.swap_x(line.done(value), k))
            held["mine"] = line.done(grad_product(line.pin(half), [turned[0]], pieces, [got[0]], [F32])[0])

        def over_y():
            total = line.pin(held["mine"])
            for v in held["x"]:
                total = total + v.astype(F32)
            total = line.done(total)
            held["own"] = lax.dynamic_index_in_dim(total, g.y, 0, keepdims=False)
            held["y"] = [
                g.swap_y(lax.dynamic_index_in_dim(total, g.y ^ ky, 0, keepdims=False).astype(BF16), ky)
                for ky in range(1, g.ny)
            ]

        def finish():
            value = line.pin(held["own"])
            for v in held["y"]:
                value = value + v.astype(F32)
            grads[e] = line.done(value * float(row_count * dp_count) ** (-0.5))

        return over_core, over_x, over_y, finish

    state = {"out": None}

    def return_rows(r):
        grad, placed, placed_at, across = {}, [], [], {}
        pieces = [slopes[r, e] for e in range(ne)]

        def multiply(k):
            weights = [proj_weight] if k == 0 else [x_weight[i, k] for i in range(len(loads))]
            grad[k] = line.done(return_product([line.pin(pieces[0])] + pieces[1:], weights))

        def others():
            for k in xs:
                multiply(k)
                grad[k] = g.swap_x(grad[k], k)

        def own():
            multiply(0)

        def keep_piece(piece, k, ky, kc):
            placed.append(piece.reshape(r_blocks, BLOCK, width))
            placed_at.append((g.d ^ (ky * g.nc + kc), (g.x ^ k) * x_blocks + r * r_blocks))

        def everywhere(k):
            piece = lax.all_gather(line.pin(grad[k]), "dp", axis=0, tiled=True)
            placed.append(piece.reshape(dp_count * r_blocks, BLOCK, width))
            placed_at.extend((s, (g.x ^ k) * x_blocks + r * r_blocks) for s in range(dp_count))

        def far(k):
            piece = line.pin(grad[k])
            across[k] = [g.swap_y(piece, ky) for ky in range(1, g.ny)]
            keep_piece(piece, k, 0, 0)
            keep_piece(g.swap_core(piece), k, 0, 1)

        def near(k):
            for ky in range(1, g.ny):
                piece = line.pin(across[k][ky - 1])
                keep_piece(piece, k, ky, 0)
                keep_piece(g.swap_core(piece), k, ky, 1)

        def place():
            sources = jnp.stack(
                [lax.dynamic_slice(tables, (s, 0, t), (1, 2, r_blocks))[0] for s, t in placed_at]
            )
            owner, offset = sources[:, 0].reshape(-1), sources[:, 1].reshape(-1)
            pieces = [line.pin(placed[0])] + placed[1:]
            state["out"] = line.done(
                place_blocks(state["out"], pieces, owner, offset, taken, g.d[None], out_blocks, width)
            )

        return others, own, everywhere, far, near, place

    load_weight(0)
    tables = lax.all_gather(jnp.stack([block_owner, block_offset]), "dp", axis=0)
    own_rows[0] = line.done(rows_at(thinker_rows, g.x * x_rows, r_rows))
    load_rows(0)
    mine = line.pin(tables[:, 0]) == g.d
    reached = mine[:, :, None] & (tables[:, 1][:, :, None] == jnp.arange(out_blocks))
    taken = line.done(jnp.any(reached, axis=(0, 1)).astype(jnp.int32))
    share_far(0)
    line.done(x_weight[0, xs[0]][0] if xs else taken)
    for r in range(1, nr):
        load_rows(r)
    for r in range(1, nr):
        own_rows[r] = rows_at(thinker_rows, line.pin(g.x) * x_rows + r * r_rows, r_rows)
    line.done(own_rows[-1])
    turn(0, rows_at(thinker_rows, line.pin(g.x) * x_rows, x_rows))
    own_weight[0] = line.done(line.pin(proj_weight[:, spans[0][0] : spans[0][1]]))
    share_near(0)

    chunks = [(r, e) for e in range(2) for r in range(nr)] + [(r, e) for r in range(nr) for e in range(2, ne)]
    hop_count = g.nz - 1
    ticks = len(chunks) + hop_count - 1

    def own_columns(e):
        own_weight[e] = line.done(line.pin(proj_weight[:, spans[e][0] : spans[e][1]]))

    def turn_others():
        for k in xs:
            turn(k, jnp.concatenate([line.pin(x_rows_got[0, k])] + [x_rows_got[r, k] for r in range(1, nr)], axis=0))

    partial_of(*chunks[0])
    load_weight(1)
    if len(chunks) > 1:
        partial_of(*chunks[1])
    at(0, lambda: own_columns(1))
    at(0, lambda: load_weight(2))
    at(0, lambda: share_far(1))
    at(0, lambda: share_near(1))
    at(1, lambda: share_far(2))
    at(1, lambda: [own_columns(e) for e in range(2, ne)])
    at(2, turn_others)
    at(2, lambda: share_near(2))
    last_row = nr - 1
    tail, overs, ends = [], [], []
    for tick in range(ticks):
        for h in range(1, hop_count):
            if 0 <= tick - h + 1 < len(chunks):
                hop(*chunks[tick - h + 1], h)
        ready = tick - hop_count + 1
        if 0 <= ready < len(chunks):
            r, e = chunks[ready]
            slope_of(r, e)
        if tick == ticks - 1:
            break
        for step in later.pop(tick, []):
            step()
        if tick + 2 < len(chunks):
            partial_of(*chunks[tick + 2])
        if 0 <= ready < len(chunks):
            if all((r, j) in slopes for j in range(ne)) and r < last_row:
                others, own, everywhere, far, near, place = return_rows(r)
                others()
                own()
                everywhere(0)
                tail.append((far, near, place))
            if all((j, e) in slopes for j in range(nr)) and ready < len(chunks) - 1:
                over_core, over_x, over_y, finish = weight_grad(e)
                over_core()
                if tick + 3 < ticks:
                    at(tick + 1, over_x)
                    at(tick + 3, over_y)
                    if tick + 4 < ticks - 1:
                        at(tick + 4, finish)
                    else:
                        ends.append(finish)
                else:
                    at(min(tick + 1, ticks - 1), over_x)
                    overs.append(over_y)
                    ends.append(finish)

    others, own, everywhere, far, near, place = return_rows(last_row)
    over_core, over_x, over_y, finish = weight_grad(ne - 1)
    PACE[0] = TAIL
    others()
    for early_far, _, _ in tail:
        for k in xs:
            early_far(k)
    own()
    far(0)
    over_core()
    for step in later.pop(ticks - 1, []):
        step()
    over_x()
    for k in xs:
        far(k)
    for step in overs:
        step()
    for _, early_near, _ in tail:
        for k in xs:
            early_near(k)
    near(0)
    over_y()
    for step in ends:
        step()
    for _, _, early_place in tail:
        early_place()
    for k in xs:
        near(k)
    finish()
    place()
    PACE[0] = COST

    return state["out"].reshape(out_blocks * BLOCK, width), jnp.concatenate(grads, axis=1)


def solution(mesh):
    return jax.shard_map(
        shards,
        mesh=mesh,
        in_specs=(P("dp", "tensor"), P("tensor", None), P(), P("dp", None), P("dp"), P("dp")),
        out_specs=(P("dp", "tensor"), P(("tensor", "dp"), None)),
        check_vma=False,
    )
```

```python
import jax
import jax.numpy as jnp
from jax import lax
from jax.experimental import pallas as pl
from jax.experimental.pallas import tpu as pltpu
from jax.sharding import PartitionSpec as P

BLOCK = 128
LANES = 256
F32 = jnp.float32
BF16 = jnp.bfloat16
CUTS = (4 / 14, 8 / 14, 11 / 14)
GATHERED = 1
COST = 0.1
TAIL = 8.0


class Grid:
    def __init__(self, tensor_count, dp_count):
        self.nx = 1 << ((tensor_count.bit_length() - 1) // 2)
        self.nz = tensor_count // self.nx
        self.nc = 2
        self.ny = dp_count // self.nc
        t, d = lax.axis_index("tensor"), lax.axis_index("dp")
        self.z, self.x = t // self.nx, t % self.nx
        self.y, self.c = d // self.nc, d % self.nc
        self.d = d

    def swap_x(self, value, k):
        pairs = [(z * self.nx + x, z * self.nx + (x ^ k)) for z in range(self.nz) for x in range(self.nx)]
        return lax.ppermute(value, "tensor", pairs)

    def hop_z(self, value, h):
        moves = [(h, h + 1), (self.nz - 1 - h, self.nz - 2 - h)]
        pairs = [(a * self.nx + x, b * self.nx + x) for a, b in moves for x in range(self.nx)]
        return lax.ppermute(value, "tensor", pairs)

    def swap_y(self, value, k):
        pairs = [(y * self.nc + c, (y ^ k) * self.nc + c) for y in range(self.ny) for c in range(self.nc)]
        return lax.ppermute(value, "dp", pairs)

    def swap_core(self, value):
        return lax.ppermute(value, "dp", [(d, d ^ 1) for d in range(self.ny * self.nc)])


def rows_at(value, start, count):
    return lax.dynamic_slice_in_dim(value, start, count, 0)


SMALL = pl.CostEstimate(flops=1000, bytes_accessed=1000, transcendentals=0)


PACE = [COST]


def work(flops):
    return pl.CostEstimate(flops=int(PACE[0] * flops), bytes_accessed=1000, transcendentals=0)


PARAMS = pltpu.CompilerParams(vmem_limit_bytes=24 << 20)


def partial_product(rows, weights, starts, size):
    count, (height, width) = len(rows), rows[0].shape

    def kernel(*refs):
        total = jnp.dot(refs[0][...], refs[count][...], preferred_element_type=F32)
        for k in range(1, count):
            total += jnp.dot(refs[k][...], refs[count + k][...], preferred_element_type=F32)
        refs[-1][...] = total.astype(BF16)

    return pl.pallas_call(
        kernel,
        grid=(size // LANES,),
        out_shape=jax.ShapeDtypeStruct((height, size), BF16),
        in_specs=[pl.BlockSpec((height, width), lambda j: (0, 0))] * count
        + [pl.BlockSpec((width, LANES), lambda j, u=s // LANES: (0, u + j)) for s in starts],
        out_specs=pl.BlockSpec((height, LANES), lambda j: (0, j)),
        compiler_params=PARAMS,
        cost_estimate=work(2 * count * height * width * size),
        name="partial_product",
    )(*rows, *weights)


def return_product(slopes, weights):
    count, height = len(slopes), slopes[0].shape[0]
    sizes = [s.shape[1] for s in slopes]
    width = weights[0].shape[0]
    tile = min(LANES, width)
    places, at = [], 0
    for i, w in enumerate(weights):
        places += [(i, at, c) for c in (0,)]
        at += w.shape[1]

    def columns(refs, start, size):
        for i, first, _ in places:
            if first <= start < first + weights[i].shape[1]:
                return refs[count + i][:, start - first : start - first + size]

    def kernel(*refs):
        total, start = None, 0
        for i, size in enumerate(sizes):
            weight = columns(refs, start, size)
            term = lax.dot_general(refs[i][...], weight, (((1,), (1,)), ((), ())), preferred_element_type=F32)
            total = term if total is None else total + term
            start += size
        refs[-1][...] = total.astype(BF16)

    return pl.pallas_call(
        kernel,
        grid=(width // tile,),
        out_shape=jax.ShapeDtypeStruct((height, width), BF16),
        in_specs=[pl.BlockSpec((height, size), lambda j: (0, 0)) for size in sizes]
        + [pl.BlockSpec((tile, w.shape[1]), lambda j: (j, 0)) for w in weights],
        out_specs=pl.BlockSpec((height, tile), lambda j: (0, j)),
        compiler_params=PARAMS,
        cost_estimate=work(2 * height * width * sum(sizes)),
        name="return_product",
    )(*slopes, *weights)


def grad_product(half, turned, slopes, extra, kinds):
    groups, count = len(turned), len(slopes)
    height, size = slopes[0].shape
    ny, nc, share, rows = turned[0].shape
    more = 0 if extra is None else groups

    def kernel(half_ref, *refs):
        pieces = refs[groups : groups + count]
        for k in range(groups):
            left = refs[k][...].reshape(ny * share, rows)
            total = None
            for i in range(count):
                term = jnp.dot(left[:, i * height : (i + 1) * height], pieces[i][...], preferred_element_type=F32)
                total = term if total is None else total + term
            total = total.reshape(ny, share, LANES)
            if more:
                total = total + refs[groups + count + k][...].astype(F32)
            out = refs[groups + count + more + k]
            out[...] = total.astype(out.dtype)

    column = pl.BlockSpec((ny, share, LANES), lambda j, h: (0, 0, j))
    return pl.pallas_call(
        kernel,
        grid_spec=pltpu.PrefetchScalarGridSpec(
            num_scalar_prefetch=1,
            grid=(size // LANES,),
            in_specs=[pl.BlockSpec((ny, None, share, rows), lambda j, h: (0, h[0], 0, 0))] * groups
            + [pl.BlockSpec((height, LANES), lambda j, h: (0, j))] * count
            + [column] * more,
            out_specs=[column] * groups,
        ),
        out_shape=[jax.ShapeDtypeStruct((ny, share, size), kind) for kind in kinds],
        compiler_params=PARAMS,
        cost_estimate=work(2 * groups * ny * share * rows * size),
        name="grad_product",
    )(half, *turned, *slopes, *([] if extra is None else extra))


def place_blocks(out, pieces, owner, offset, taken, me, out_blocks, width):
    where = [(i, j) for i, piece in enumerate(pieces) for j in range(piece.shape[0])]
    count, total = len(pieces), len(where)
    first = out is None

    def kernel(owner_ref, offset_ref, taken_ref, me_ref, *refs):
        sources, (out_ref, stage, zero, in_sems, out_sems, zero_sems) = refs[:count], refs[-6:]
        mine = me_ref[0]

        def arrive(n):
            i, j = where[n]
            return pltpu.make_async_copy(sources[i].at[j], stage.at[n], in_sems.at[n])

        def leave(n):
            return pltpu.make_async_copy(stage.at[n], out_ref.at[offset_ref[n]], out_sems.at[n])

        def clear(n):
            return pltpu.make_async_copy(zero, out_ref.at[n], zero_sems.at[n])

        def each(work):
            for n in range(total):
                pl.when(owner_ref[n] == mine)(lambda: work(n))

        def forward(n):
            arrive(n).wait()
            leave(n).start()

        each(lambda n: arrive(n).start())
        if first:
            zero[...] = jnp.zeros_like(zero)
            for n in range(out_blocks):
                pl.when(taken_ref[n] == 0)(lambda: clear(n).start())
        each(forward)
        each(lambda n: leave(n).wait())
        if first:
            for n in range(out_blocks):
                pl.when(taken_ref[n] == 0)(lambda: clear(n).wait())

    smem = pl.BlockSpec(memory_space=pltpu.SMEM)
    hbm = pl.BlockSpec(memory_space=pl.ANY)
    before = [] if first else [out]
    return pl.pallas_call(
        kernel,
        out_shape=jax.ShapeDtypeStruct((out_blocks, BLOCK, width), BF16),
        in_specs=[smem] * 4 + [hbm] * (count + len(before)),
        out_specs=hbm,
        scratch_shapes=[
            pltpu.VMEM((total, BLOCK, width), BF16),
            pltpu.VMEM((BLOCK, width), BF16),
            pltpu.SemaphoreType.DMA((total,)),
            pltpu.SemaphoreType.DMA((total,)),
            pltpu.SemaphoreType.DMA((out_blocks,)),
        ],
        input_output_aliases={} if first else {4 + count: 0},
        compiler_params=PARAMS,
        cost_estimate=SMALL,
        name="place_blocks",
    )(owner, offset, taken, me, *pieces, *before)


class Order:
    def __init__(self):
        self.last = None

    def pin(self, value):
        if self.last is not None:
            value, _ = lax.optimization_barrier((value, self.last))
        return value

    def done(self, value):
        self.last = value
        return value


def shards(thinker_rows, proj_weight, proj_bias, cotangent, block_owner, block_offset):
    g = Grid(lax.axis_size("tensor"), lax.axis_size("dp"))
    row_count, width = thinker_rows.shape
    dp_count = g.ny * g.nc
    out_width = proj_weight.shape[1]
    x_rows = row_count // g.nx
    x_blocks = x_rows // BLOCK
    nr = min(2, x_blocks)
    r_rows = x_rows // nr
    r_blocks = r_rows // BLOCK
    units = out_width // LANES
    ends = [0] + [round(units * f) * LANES for f in CUTS] + [out_width]
    spans = list(zip(ends[:-1], ends[1:]))
    ne = len(spans)
    loads = [spans[0], spans[1], (spans[2][0], out_width)]
    share = width // dp_count
    xs = range(1, g.nx)
    out_blocks = 2 * row_count // BLOCK
    line = Order()
    later = {}

    def at(tick, work):
        later.setdefault(tick, []).append(work)

    x_weight, x_rows_got = {}, {}

    def load_of(e):
        return min(e, len(loads) - 1)

    def load_weight(i):
        start, end = loads[i]
        mine = lax.dynamic_slice(proj_weight, (line.pin(g.d * share), start), (share, end - start))
        for k in xs:
            x_weight[i, k] = g.swap_x(mine, k)

    def share_far(i):
        for k in xs:
            got = line.pin(x_weight[i, k])
            parts = {ky * g.nc: g.swap_y(got, ky) for ky in range(1, g.ny)}
            parts[0], parts[1] = got, g.swap_core(got)
            x_weight[i, k] = parts

    def share_near(i):
        for k in xs:
            parts = x_weight[i, k]
            for ky in range(1, g.ny):
                key = ky * g.nc
                parts[key] = line.pin(parts[key])
                parts[key + 1] = g.swap_core(parts[key])
            full = jnp.zeros((width, loads[i][1] - loads[i][0]), BF16)
            for key, part in sorted(parts.items()):
                full = lax.dynamic_update_slice(full, part, ((g.d ^ key) * share, 0))
            x_weight[i, k] = line.done(full)

    def share_all(i):
        for k in xs:
            x_weight[i, k] = lax.all_gather(line.pin(x_weight[i, k]), "dp", axis=0, tiled=True)

    def load_rows(r):
        for k in xs:
            if r:
                mine = rows_at(thinker_rows, (line.pin(g.x) ^ k) * x_rows + r * r_rows, r_rows)
            else:
                blocks = thinker_rows.reshape(-1, r_rows, width)
                mine = lax.dynamic_index_in_dim(blocks, (g.x ^ k) * nr, 0, keepdims=False)
            x_rows_got[r, k] = g.swap_x(mine, k)

    own_rows = [None] * nr
    own_weight = [None] * ne
    turned = {}

    def turn(k, value):
        turned[k] = line.done(value.T.reshape(g.ny, g.nc, share, x_rows))

    def add_up(part, got):
        return line.done((line.pin(part).astype(F32) + got.astype(F32)).astype(BF16))

    partials, hops, slopes = {}, {}, {}

    def partial_of(r, e):
        start, end = spans[e]
        rows = [line.pin(own_rows[r])] + [x_rows_got[r, k] for k in xs]
        i = load_of(e)
        weights = [own_weight[e]] + [x_weight[i, k] for k in xs]
        part = line.done(partial_product(rows, weights, [0] + [start - loads[i][0]] * len(xs), end - start))
        partials[r, e] = part
        hops[r, e] = [g.hop_z(part, 0)]

    def hop(r, e, h):
        hops[r, e].append(g.hop_z(add_up(partials[r, e], hops[r, e][-1]), h))

    def slope_of(r, e):
        start, end = spans[e]
        total = line.pin(partials[r, e]).astype(F32)
        for got in hops[r, e]:
            total = total + got.astype(F32)
        pre_act = total + proj_bias[start:end]
        gate = jax.nn.sigmoid(pre_act)
        cot = lax.dynamic_slice(cotangent, (g.x * x_rows + r * r_rows, start), (r_rows, end - start))
        slopes[r, e] = line.done((cot.astype(F32) * gate * (1.0 + pre_act * (1.0 - gate))).astype(BF16))

    grads = [None] * ne
    half = g.c.astype(jnp.int32)[None]

    def weight_grad(e):
        pieces = [slopes[r, e] for r in range(nr)]
        groups = list(xs) + [0]
        held = {}

        def over_core():
            give = grad_product(
                1 - half, [turned[k] for k in groups], [line.pin(pieces[0])] + pieces[1:], None, [BF16] * g.nx
            )
            line.done(give[0])
            held["core"] = {k: g.swap_core(v) for k, v in zip(groups, give)}

        def over_x():
            got = held["core"]
            held["x"] = []
            for k in xs:
                value = grad_product(line.pin(half), [turned[k]], pieces, [got[k]], [BF16])[0]
                held["x"].append(g.swap_x(line.done(value), k))
            held["mine"] = line.done(grad_product(line.pin(half), [turned[0]], pieces, [got[0]], [F32])[0])

        def over_y():
            total = line.pin(held["mine"])
            for v in held["x"]:
                total = total + v.astype(F32)
            total = line.done(total)
            held["own"] = lax.dynamic_index_in_dim(total, g.y, 0, keepdims=False)
            held["y"] = [
                g.swap_y(lax.dynamic_index_in_dim(total, g.y ^ ky, 0, keepdims=False).astype(BF16), ky)
                for ky in range(1, g.ny)
            ]

        def finish():
            value = line.pin(held["own"])
            for v in held["y"]:
                value = value + v.astype(F32)
            grads[e] = line.done(value * float(row_count * dp_count) ** (-0.5))

        return over_core, over_x, over_y, finish

    state = {"out": None}

    def return_rows(r):
        grad, placed, placed_at, across = {}, [], [], {}
        pieces = [slopes[r, e] for e in range(ne)]

        def multiply(k):
            weights = [proj_weight] if k == 0 else [x_weight[i, k] for i in range(len(loads))]
            grad[k] = line.done(return_product([line.pin(pieces[0])] + pieces[1:], weights))

        def others():
            for k in xs:
                multiply(k)
                grad[k] = g.swap_x(grad[k], k)

        def own():
            multiply(0)

        def keep_piece(piece, k, ky, kc):
            placed.append(piece.reshape(r_blocks, BLOCK, width))
            placed_at.append((g.d ^ (ky * g.nc + kc), (g.x ^ k) * x_blocks + r * r_blocks))

        def everywhere(k):
            piece = lax.all_gather(line.pin(grad[k]), "dp", axis=0, tiled=True)
            placed.append(piece.reshape(dp_count * r_blocks, BLOCK, width))
            placed_at.extend((s, (g.x ^ k) * x_blocks + r * r_blocks) for s in range(dp_count))

        def far(k):
            piece = line.pin(grad[k])
            across[k] = [g.swap_y(piece, ky) for ky in range(1, g.ny)]
            keep_piece(piece, k, 0, 0)
            keep_piece(g.swap_core(piece), k, 0, 1)

        def near(k):
            for ky in range(1, g.ny):
                piece = line.pin(across[k][ky - 1])
                keep_piece(piece, k, ky, 0)
                keep_piece(g.swap_core(piece), k, ky, 1)

        def place():
            sources = jnp.stack(
                [lax.dynamic_slice(tables, (s, 0, t), (1, 2, r_blocks))[0] for s, t in placed_at]
            )
            owner, offset = sources[:, 0].reshape(-1), sources[:, 1].reshape(-1)
            pieces = [line.pin(placed[0])] + placed[1:]
            state["out"] = line.done(
                place_blocks(state["out"], pieces, owner, offset, taken, g.d[None], out_blocks, width)
            )

        return others, own, everywhere, far, near, place

    load_weight(0)
    tables = lax.all_gather(jnp.stack([block_owner, block_offset]), "dp", axis=0)
    own_rows[0] = line.done(rows_at(thinker_rows, g.x * x_rows, r_rows))
    load_rows(0)
    mine = line.pin(tables[:, 0]) == g.d
    reached = mine[:, :, None] & (tables[:, 1][:, :, None] == jnp.arange(out_blocks))
    taken = line.done(jnp.any(reached, axis=(0, 1)).astype(jnp.int32))
    share_far(0)
    line.done(x_weight[0, xs[0]][0] if xs else taken)
    for r in range(1, nr):
        load_rows(r)
    for r in range(1, nr):
        own_rows[r] = rows_at(thinker_rows, line.pin(g.x) * x_rows + r * r_rows, r_rows)
    line.done(own_rows[-1])
    turn(0, rows_at(thinker_rows, line.pin(g.x) * x_rows, x_rows))
    own_weight[0] = line.done(line.pin(proj_weight[:, spans[0][0] : spans[0][1]]))
    share_near(0)

    chunks = [(r, e) for e in range(2) for r in range(nr)] + [(r, e) for r in range(nr) for e in range(2, ne)]
    hop_count = g.nz - 1
    ticks = len(chunks) + hop_count - 1

    def own_columns(e):
        own_weight[e] = line.done(line.pin(proj_weight[:, spans[e][0] : spans[e][1]]))

    def turn_others():
        for k in xs:
            turn(k, jnp.concatenate([line.pin(x_rows_got[0, k])] + [x_rows_got[r, k] for r in range(1, nr)], axis=0))

    partial_of(*chunks[0])
    load_weight(1)
    if len(chunks) > 1:
        partial_of(*chunks[1])
    at(0, lambda: own_columns(1))
    at(0, lambda: load_weight(2))
    at(0, lambda: share_far(1))
    at(0, lambda: share_near(1))
    at(1, lambda: share_far(2))
    at(1, lambda: [own_columns(e) for e in range(2, ne)])
    at(2, turn_others)
    last_row = nr - 1
    tail, overs, ends = [], [], []
    for tick in range(ticks):
        if 1 <= tick and tick + 1 < len(chunks):
            if tick == 3:
                share_near(2)
            partial_of(*chunks[tick + 1])
        for h in range(1, hop_count):
            if 0 <= tick - h + 1 < len(chunks):
                hop(*chunks[tick - h + 1], h)
        ready = tick - hop_count + 1
        if 0 <= ready < len(chunks):
            r, e = chunks[ready]
            slope_of(r, e)
        if tick == ticks - 1:
            break
        for step in later.pop(tick, []):
            step()
        if 0 <= ready < len(chunks):
            if all((r, j) in slopes for j in range(ne)) and r < last_row:
                others, own, everywhere, far, near, place = return_rows(r)
                others()
                own()
                everywhere(0)
                tail.append((far, near, place))
            if all((j, e) in slopes for j in range(nr)) and ready < len(chunks) - 1:
                over_core, over_x, over_y, finish = weight_grad(e)
                over_core()
                if tick + 3 < ticks:
                    at(tick + 1, over_x)
                    at(tick + 3, over_y)
                    if tick + 4 < ticks - 1:
                        at(tick + 4, finish)
                    else:
                        ends.append(finish)
                else:
                    at(min(tick + 1, ticks - 1), over_x)
                    overs.append(over_y)
                    ends.append(finish)

    others, own, everywhere, far, near, place = return_rows(last_row)
    over_core, over_x, over_y, finish = weight_grad(ne - 1)
    PACE[0] = TAIL
    for early_far, _, _ in tail:
        for k in xs:
            early_far(k)
    others()
    own()
    if len(ends) > 1:
        ends.pop(0)()
    far(0)
    over_core()
    for step in later.pop(ticks - 1, []):
        step()
    over_x()
    for k in xs:
        far(k)
    for step in overs:
        step()
    for _, early_near, _ in tail:
        for k in xs:
            early_near(k)
    near(0)
    over_y()
    for _, _, early_place in tail:
        early_place()
    for k in xs:
        near(k)
    place()
    for step in ends:
        step()
    finish()
    PACE[0] = COST

    return state["out"].reshape(out_blocks * BLOCK, width), jnp.concatenate(grads, axis=1)


def solution(mesh):
    return jax.shard_map(
        shards,
        mesh=mesh,
        in_specs=(P("dp", "tensor"), P("tensor", None), P(), P("dp", None), P("dp"), P("dp")),
        out_specs=(P("dp", "tensor"), P(("tensor", "dp"), None)),
        check_vma=False,
    )
```

```python
import jax
import jax.numpy as jnp
from jax import lax
from jax.experimental import pallas as pl
from jax.experimental.pallas import tpu as pltpu
from jax.sharding import PartitionSpec as P

BLOCK = 128
LANES = 256
F32 = jnp.float32
BF16 = jnp.bfloat16
CUTS = (4 / 14, 8 / 14, 11 / 14)
GATHERED = 1
COST = 0.1
TAIL = 8.0


class Grid:
    def __init__(self, tensor_count, dp_count):
        self.nx = 1 << ((tensor_count.bit_length() - 1) // 2)
        self.nz = tensor_count // self.nx
        self.nc = 2
        self.ny = dp_count // self.nc
        t, d = lax.axis_index("tensor"), lax.axis_index("dp")
        self.z, self.x = t // self.nx, t % self.nx
        self.y, self.c = d // self.nc, d % self.nc
        self.d = d

    def swap_x(self, value, k):
        pairs = [(z * self.nx + x, z * self.nx + (x ^ k)) for z in range(self.nz) for x in range(self.nx)]
        return lax.ppermute(value, "tensor", pairs)

    def hop_z(self, value, h):
        moves = [(h, h + 1), (self.nz - 1 - h, self.nz - 2 - h)]
        pairs = [(a * self.nx + x, b * self.nx + x) for a, b in moves for x in range(self.nx)]
        return lax.ppermute(value, "tensor", pairs)

    def swap_y(self, value, k):
        pairs = [(y * self.nc + c, (y ^ k) * self.nc + c) for y in range(self.ny) for c in range(self.nc)]
        return lax.ppermute(value, "dp", pairs)

    def swap_core(self, value):
        return lax.ppermute(value, "dp", [(d, d ^ 1) for d in range(self.ny * self.nc)])


def rows_at(value, start, count):
    return lax.dynamic_slice_in_dim(value, start, count, 0)


SMALL = pl.CostEstimate(flops=1000, bytes_accessed=1000, transcendentals=0)


PACE = [COST]


def work(flops):
    return pl.CostEstimate(flops=int(PACE[0] * flops), bytes_accessed=1000, transcendentals=0)


PARAMS = pltpu.CompilerParams(vmem_limit_bytes=24 << 20)


def partial_product(rows, weights, starts, size):
    count, (height, width) = len(rows), rows[0].shape

    def kernel(*refs):
        total = jnp.dot(refs[0][...], refs[count][...], preferred_element_type=F32)
        for k in range(1, count):
            total += jnp.dot(refs[k][...], refs[count + k][...], preferred_element_type=F32)
        refs[-1][...] = total.astype(BF16)

    return pl.pallas_call(
        kernel,
        grid=(size // LANES,),
        out_shape=jax.ShapeDtypeStruct((height, size), BF16),
        in_specs=[pl.BlockSpec((height, width), lambda j: (0, 0))] * count
        + [pl.BlockSpec((width, LANES), lambda j, u=s // LANES: (0, u + j)) for s in starts],
        out_specs=pl.BlockSpec((height, LANES), lambda j: (0, j)),
        compiler_params=PARAMS,
        cost_estimate=work(2 * count * height * width * size),
        name="partial_product",
    )(*rows, *weights)


def return_product(slopes, weights):
    count, height = len(slopes), slopes[0].shape[0]
    sizes = [s.shape[1] for s in slopes]
    width = weights[0].shape[0]
    tile = min(LANES, width)
    places, at = [], 0
    for i, w in enumerate(weights):
        places += [(i, at, c) for c in (0,)]
        at += w.shape[1]

    def columns(refs, start, size):
        for i, first, _ in places:
            if first <= start < first + weights[i].shape[1]:
                return refs[count + i][:, start - first : start - first + size]

    def kernel(*refs):
        total, start = None, 0
        for i, size in enumerate(sizes):
            weight = columns(refs, start, size)
            term = lax.dot_general(refs[i][...], weight, (((1,), (1,)), ((), ())), preferred_element_type=F32)
            total = term if total is None else total + term
            start += size
        refs[-1][...] = total.astype(BF16)

    return pl.pallas_call(
        kernel,
        grid=(width // tile,),
        out_shape=jax.ShapeDtypeStruct((height, width), BF16),
        in_specs=[pl.BlockSpec((height, size), lambda j: (0, 0)) for size in sizes]
        + [pl.BlockSpec((tile, w.shape[1]), lambda j: (j, 0)) for w in weights],
        out_specs=pl.BlockSpec((height, tile), lambda j: (0, j)),
        compiler_params=PARAMS,
        cost_estimate=work(2 * height * width * sum(sizes)),
        name="return_product",
    )(*slopes, *weights)


def grad_product(half, turned, slopes, extra, kinds):
    groups, count = len(turned), len(slopes)
    height, size = slopes[0].shape
    ny, nc, share, rows = turned[0].shape
    more = 0 if extra is None else groups

    def kernel(half_ref, *refs):
        pieces = refs[groups : groups + count]
        for k in range(groups):
            left = refs[k][...].reshape(ny * share, rows)
            total = None
            for i in range(count):
                term = jnp.dot(left[:, i * height : (i + 1) * height], pieces[i][...], preferred_element_type=F32)
                total = term if total is None else total + term
            total = total.reshape(ny, share, LANES)
            if more:
                total = total + refs[groups + count + k][...].astype(F32)
            out = refs[groups + count + more + k]
            out[...] = total.astype(out.dtype)

    column = pl.BlockSpec((ny, share, LANES), lambda j, h: (0, 0, j))
    return pl.pallas_call(
        kernel,
        grid_spec=pltpu.PrefetchScalarGridSpec(
            num_scalar_prefetch=1,
            grid=(size // LANES,),
            in_specs=[pl.BlockSpec((ny, None, share, rows), lambda j, h: (0, h[0], 0, 0))] * groups
            + [pl.BlockSpec((height, LANES), lambda j, h: (0, j))] * count
            + [column] * more,
            out_specs=[column] * groups,
        ),
        out_shape=[jax.ShapeDtypeStruct((ny, share, size), kind) for kind in kinds],
        compiler_params=PARAMS,
        cost_estimate=work(2 * groups * ny * share * rows * size),
        name="grad_product",
    )(half, *turned, *slopes, *([] if extra is None else extra))


def place_blocks(out, pieces, owner, offset, taken, me, out_blocks, width):
    where = [(i, j) for i, piece in enumerate(pieces) for j in range(piece.shape[0])]
    count, total = len(pieces), len(where)
    first = out is None

    def kernel(owner_ref, offset_ref, taken_ref, me_ref, *refs):
        sources, (out_ref, stage, zero, in_sems, out_sems, zero_sems) = refs[:count], refs[-6:]
        mine = me_ref[0]

        def arrive(n):
            i, j = where[n]
            return pltpu.make_async_copy(sources[i].at[j], stage.at[n], in_sems.at[n])

        def leave(n):
            return pltpu.make_async_copy(stage.at[n], out_ref.at[offset_ref[n]], out_sems.at[n])

        def clear(n):
            return pltpu.make_async_copy(zero, out_ref.at[n], zero_sems.at[n])

        def each(work):
            for n in range(total):
                pl.when(owner_ref[n] == mine)(lambda: work(n))

        def forward(n):
            arrive(n).wait()
            leave(n).start()

        each(lambda n: arrive(n).start())
        if first:
            zero[...] = jnp.zeros_like(zero)
            for n in range(out_blocks):
                pl.when(taken_ref[n] == 0)(lambda: clear(n).start())
        each(forward)
        each(lambda n: leave(n).wait())
        if first:
            for n in range(out_blocks):
                pl.when(taken_ref[n] == 0)(lambda: clear(n).wait())

    smem = pl.BlockSpec(memory_space=pltpu.SMEM)
    hbm = pl.BlockSpec(memory_space=pl.ANY)
    before = [] if first else [out]
    return pl.pallas_call(
        kernel,
        out_shape=jax.ShapeDtypeStruct((out_blocks, BLOCK, width), BF16),
        in_specs=[smem] * 4 + [hbm] * (count + len(before)),
        out_specs=hbm,
        scratch_shapes=[
            pltpu.VMEM((total, BLOCK, width), BF16),
            pltpu.VMEM((BLOCK, width), BF16),
            pltpu.SemaphoreType.DMA((total,)),
            pltpu.SemaphoreType.DMA((total,)),
            pltpu.SemaphoreType.DMA((out_blocks,)),
        ],
        input_output_aliases={} if first else {4 + count: 0},
        compiler_params=PARAMS,
        cost_estimate=SMALL,
        name="place_blocks",
    )(owner, offset, taken, me, *pieces, *before)


class Order:
    def __init__(self):
        self.last = None

    def pin(self, value):
        if self.last is not None:
            value, _ = lax.optimization_barrier((value, self.last))
        return value

    def done(self, value):
        self.last = value
        return value


def shards(thinker_rows, proj_weight, proj_bias, cotangent, block_owner, block_offset):
    g = Grid(lax.axis_size("tensor"), lax.axis_size("dp"))
    row_count, width = thinker_rows.shape
    dp_count = g.ny * g.nc
    out_width = proj_weight.shape[1]
    x_rows = row_count // g.nx
    x_blocks = x_rows // BLOCK
    nr = min(2, x_blocks)
    r_rows = x_rows // nr
    r_blocks = r_rows // BLOCK
    units = out_width // LANES
    ends = [0] + [round(units * f) * LANES for f in CUTS] + [out_width]
    spans = list(zip(ends[:-1], ends[1:]))
    ne = len(spans)
    loads = [spans[0], spans[1], (spans[2][0], out_width)]
    share = width // dp_count
    xs = range(1, g.nx)
    out_blocks = 2 * row_count // BLOCK
    line = Order()
    later = {}

    def at(tick, work):
        later.setdefault(tick, []).append(work)

    x_weight, x_rows_got = {}, {}

    def load_of(e):
        return min(e, len(loads) - 1)

    def load_weight(i):
        start, end = loads[i]
        mine = lax.dynamic_slice(proj_weight, (line.pin(g.d * share), start), (share, end - start))
        for k in xs:
            x_weight[i, k] = g.swap_x(mine, k)

    def share_far(i):
        for k in xs:
            got = line.pin(x_weight[i, k])
            parts = {ky * g.nc: g.swap_y(got, ky) for ky in range(1, g.ny)}
            parts[0], parts[1] = got, g.swap_core(got)
            x_weight[i, k] = parts

    def share_near(i):
        for k in xs:
            parts = x_weight[i, k]
            for ky in range(1, g.ny):
                key = ky * g.nc
                parts[key] = line.pin(parts[key])
                parts[key + 1] = g.swap_core(parts[key])
            full = jnp.zeros((width, loads[i][1] - loads[i][0]), BF16)
            for key, part in sorted(parts.items()):
                full = lax.dynamic_update_slice(full, part, ((g.d ^ key) * share, 0))
            x_weight[i, k] = line.done(full)

    def share_all(i):
        for k in xs:
            x_weight[i, k] = lax.all_gather(line.pin(x_weight[i, k]), "dp", axis=0, tiled=True)

    def load_rows(r):
        for k in xs:
            if r:
                mine = rows_at(thinker_rows, (line.pin(g.x) ^ k) * x_rows + r * r_rows, r_rows)
            else:
                blocks = thinker_rows.reshape(-1, r_rows, width)
                mine = lax.dynamic_index_in_dim(blocks, (g.x ^ k) * nr, 0, keepdims=False)
            x_rows_got[r, k] = g.swap_x(mine, k)

    own_rows = [None] * nr
    own_weight = [None] * ne
    turned = {}

    def turn(k, value):
        turned[k] = line.done(value.T.reshape(g.ny, g.nc, share, x_rows))

    def add_up(part, got):
        return line.done((line.pin(part).astype(F32) + got.astype(F32)).astype(BF16))

    partials, hops, slopes = {}, {}, {}

    def partial_of(r, e):
        start, end = spans[e]
        rows = [line.pin(own_rows[r])] + [x_rows_got[r, k] for k in xs]
        i = load_of(e)
        weights = [own_weight[e]] + [x_weight[i, k] for k in xs]
        part = line.done(partial_product(rows, weights, [0] + [start - loads[i][0]] * len(xs), end - start))
        partials[r, e] = part
        hops[r, e] = [g.hop_z(part, 0)]

    def hop(r, e, h):
        hops[r, e].append(g.hop_z(add_up(partials[r, e], hops[r, e][-1]), h))

    def slope_of(r, e):
        start, end = spans[e]
        total = line.pin(partials[r, e]).astype(F32)
        for got in hops[r, e]:
            total = total + got.astype(F32)
        pre_act = total + proj_bias[start:end]
        gate = jax.nn.sigmoid(pre_act)
        cot = lax.dynamic_slice(cotangent, (g.x * x_rows + r * r_rows, start), (r_rows, end - start))
        slopes[r, e] = line.done((cot.astype(F32) * gate * (1.0 + pre_act * (1.0 - gate))).astype(BF16))

    grads = [None] * ne
    half = g.c.astype(jnp.int32)[None]

    def weight_grad(e):
        pieces = [slopes[r, e] for r in range(nr)]
        groups = list(xs) + [0]
        held = {}

        def over_core():
            give = grad_product(
                1 - half, [turned[k] for k in groups], [line.pin(pieces[0])] + pieces[1:], None, [BF16] * g.nx
            )
            line.done(give[0])
            held["core"] = {k: g.swap_core(v) for k, v in zip(groups, give)}

        def over_x():
            got = held["core"]
            held["x"] = []
            for k in xs:
                value = grad_product(line.pin(half), [turned[k]], pieces, [got[k]], [BF16])[0]
                held["x"].append(g.swap_x(line.done(value), k))
            held["mine"] = line.done(grad_product(line.pin(half), [turned[0]], pieces, [got[0]], [F32])[0])

        def over_y():
            total = line.pin(held["mine"])
            for v in held["x"]:
                total = total + v.astype(F32)
            total = line.done(total)
            held["own"] = lax.dynamic_index_in_dim(total, g.y, 0, keepdims=False)
            held["y"] = [
                g.swap_y(lax.dynamic_index_in_dim(total, g.y ^ ky, 0, keepdims=False).astype(BF16), ky)
                for ky in range(1, g.ny)
            ]

        def finish():
            value = line.pin(held["own"])
            for v in held["y"]:
                value = value + v.astype(F32)
            grads[e] = line.done(value * float(row_count * dp_count) ** (-0.5))

        return over_core, over_x, over_y, finish

    state = {"out": None}

    def return_rows(r):
        grad, placed, placed_at, across = {}, [], [], {}
        pieces = [slopes[r, e] for e in range(ne)]

        def multiply(k):
            weights = [proj_weight] if k == 0 else [x_weight[i, k] for i in range(len(loads))]
            grad[k] = line.done(return_product([line.pin(pieces[0])] + pieces[1:], weights))

        def others():
            for k in xs:
                multiply(k)
                grad[k] = g.swap_x(grad[k], k)

        def own():
            multiply(0)

        def keep_piece(piece, k, ky, kc):
            placed.append(piece.reshape(r_blocks, BLOCK, width))
            placed_at.append((g.d ^ (ky * g.nc + kc), (g.x ^ k) * x_blocks + r * r_blocks))

        def everywhere(k):
            piece = lax.all_gather(line.pin(grad[k]), "dp", axis=0, tiled=True)
            placed.append(piece.reshape(dp_count * r_blocks, BLOCK, width))
            placed_at.extend((s, (g.x ^ k) * x_blocks + r * r_blocks) for s in range(dp_count))

        def far(k):
            piece = line.pin(grad[k])
            across[k] = [g.swap_y(piece, ky) for ky in range(1, g.ny)]
            keep_piece(piece, k, 0, 0)
            keep_piece(g.swap_core(piece), k, 0, 1)

        def near(k):
            for ky in range(1, g.ny):
                piece = line.pin(across[k][ky - 1])
                keep_piece(piece, k, ky, 0)
                keep_piece(g.swap_core(piece), k, ky, 1)

        def place():
            sources = jnp.stack(
                [lax.dynamic_slice(tables, (s, 0, t), (1, 2, r_blocks))[0] for s, t in placed_at]
            )
            owner, offset = sources[:, 0].reshape(-1), sources[:, 1].reshape(-1)
            pieces = [line.pin(placed[0])] + placed[1:]
            state["out"] = line.done(
                place_blocks(state["out"], pieces, owner, offset, taken, g.d[None], out_blocks, width)
            )

        return others, own, everywhere, far, near, place

    load_weight(0)
    tables = lax.all_gather(jnp.stack([block_owner, block_offset]), "dp", axis=0)
    own_rows[0] = line.done(rows_at(thinker_rows, g.x * x_rows, r_rows))
    load_rows(0)
    mine = line.pin(tables[:, 0]) == g.d
    reached = mine[:, :, None] & (tables[:, 1][:, :, None] == jnp.arange(out_blocks))
    taken = line.done(jnp.any(reached, axis=(0, 1)).astype(jnp.int32))
    share_far(0)
    line.done(x_weight[0, xs[0]][0] if xs else taken)
    for r in range(1, nr):
        load_rows(r)
    for r in range(1, nr):
        own_rows[r] = rows_at(thinker_rows, line.pin(g.x) * x_rows + r * r_rows, r_rows)
    line.done(own_rows[-1])
    turn(0, rows_at(thinker_rows, line.pin(g.x) * x_rows, x_rows))
    own_weight[0] = line.done(line.pin(proj_weight[:, spans[0][0] : spans[0][1]]))
    share_near(0)

    chunks = [(r, e) for e in range(2) for r in range(nr)] + [(r, e) for r in range(nr) for e in range(2, ne)]
    hop_count = g.nz - 1
    ticks = len(chunks) + hop_count - 1

    def own_columns(e):
        own_weight[e] = line.done(line.pin(proj_weight[:, spans[e][0] : spans[e][1]]))

    def turn_others():
        for k in xs:
            turn(k, jnp.concatenate([line.pin(x_rows_got[0, k])] + [x_rows_got[r, k] for r in range(1, nr)], axis=0))

    partial_of(*chunks[0])
    load_weight(1)
    load_weight(2)
    if len(chunks) > 1:
        partial_of(*chunks[1])
    at(0, lambda: own_columns(1))
    at(0, lambda: share_far(1))
    at(0, lambda: share_near(1))
    at(1, lambda: share_far(2))
    at(1, lambda: [own_columns(e) for e in range(2, ne)])
    at(2, turn_others)
    last_row = nr - 1
    tail, overs, ends = [], [], []
    for tick in range(ticks):
        if 1 <= tick and tick + 1 < len(chunks):
            if tick == 3:
                share_near(2)
            partial_of(*chunks[tick + 1])
        for h in range(1, hop_count):
            if 0 <= tick - h + 1 < len(chunks):
                hop(*chunks[tick - h + 1], h)
        ready = tick - hop_count + 1
        if 0 <= ready < len(chunks):
            r, e = chunks[ready]
            slope_of(r, e)
        if tick == ticks - 1:
            break
        for step in later.pop(tick, []):
            step()
        if 0 <= ready < len(chunks):
            if all((r, j) in slopes for j in range(ne)) and r < last_row:
                others, own, everywhere, far, near, place = return_rows(r)
                others()
                own()
                far(0)
                tail.append((far, near, place))
            if all((j, e) in slopes for j in range(nr)) and ready < len(chunks) - 1:
                over_core, over_x, over_y, finish = weight_grad(e)
                over_core()
                if tick + 3 < ticks:
                    at(tick + 1, over_x)
                    at(tick + 3, over_y)
                    if tick + 4 < ticks - 1:
                        at(tick + 4, finish)
                    else:
                        ends.append(finish)
                else:
                    at(min(tick + 1, ticks - 1), over_x)
                    overs.append(over_y)
                    ends.append(finish)

    others, own, everywhere, far, near, place = return_rows(last_row)
    over_core, over_x, over_y, finish = weight_grad(ne - 1)
    PACE[0] = TAIL
    for early_far, _, _ in tail:
        for k in xs:
            early_far(k)
    others()
    own()
    if len(ends) > 1:
        ends.pop(0)()
    far(0)
    over_core()
    for step in later.pop(ticks - 1, []):
        step()
    over_x()
    for k in xs:
        far(k)
    for step in overs:
        step()
    for _, early_near, _ in tail:
        for k in range(g.nx):
            early_near(k)
    near(0)
    over_y()
    for _, _, early_place in tail:
        early_place()
    for k in xs:
        near(k)
    place()
    for step in ends:
        step()
    finish()
    PACE[0] = COST

    return state["out"].reshape(out_blocks * BLOCK, width), jnp.concatenate(grads, axis=1)


def solution(mesh):
    return jax.shard_map(
        shards,
        mesh=mesh,
        in_specs=(P("dp", "tensor"), P("tensor", None), P(), P("dp", None), P("dp"), P("dp")),
        out_specs=(P("dp", "tensor"), P(("tensor", "dp"), None)),
        check_vma=False,
    )
```
